768 devices in a mesh: gx: 96 (over y, z), gy: 8 (over x, core).
Axes of the slice: x: 4, y: 8, z: 12, core: 2. Of those that a mesh axis runs over, the one named last changes fastest.
Arguments:
- state: bfloat16 [6, 125, 393216], P(None, None, ('gx', 'gy')), may hold values from -6 to 6
- forcing: bfloat16 [6, 125, 393216], P(None, None, ('gx', 'gy')), may hold values from -6 to 6
- volume_flux_matrix: bfloat16 [125, 125], replicated, may hold values from -0.5 to 0.5
- viscous_matrix: bfloat16 [125, 125], replicated, may hold values from -0.5 to 0.5
- linear_flux_matrix: float32 [6, 6], replicated, may hold values from -2.5 to 2.5
- viscosity: float32 [393216], P(('gx', 'gy')), may hold values from 0.1 to 1
- lift: bfloat16 [6, 125, 25], replicated, may hold values from -0.5 to 0.5
- wall_flags: int32 [393216], P(('gx', 'gy')), may hold values 0 or 1
- restriction_weight: float32 [8, 125], replicated, may hold values from -0.1875 to 0.1875
- owner: int32 [393216, 1], P(('gx', 'gy')), may hold values from 0 to 7; in each aligned block of 512 rows (0 to 511, 512 to 1023, ...) at most 256 rows name the same one
- slot: int32 [393216], P(('gx', 'gy')), may hold values from 0 to 31
- coarse_inverse: float32 [48, 48, 24576], P(None, None, ('gx', 'gy')), as said below
- coupling: float32 [48, 48], replicated, may hold values from -0.4375 to 0.4375
- prolongation_weight: float32 [125, 8], replicated, may hold values from -2 to 2
Outputs:
- residual: bfloat16 [6, 125, 393216], P(None, None, ('gx', 'gy'))
- correction: bfloat16 [6, 125, 393216], P(None, None, ('gx', 'gy'))
The draws below stay inside these ranges and needn't reach their ends.
Inputs may be any that keep to these rules, and one draw needn't show every extreme that they name: `owner`: from the elements of one device at most 256 name one member, and some device gives exactly 256 elements to some member. `coarse_inverse`: one 48 x 48 block for each agglomerate.
All inputs are finite; a program needn't handle non-finite values. No bound on the sum of `wall_flags` on one device may be relied on, other than what follows from the above.
Results may differ from the reference program's by a relative error of at most 0.004.
Values may be sent and summed in bfloat16 or wider, within the bound.
No kernel may reach another device: no remote copies, remote signals or barrier semaphores. Data moves between devices by JAX's collectives and lax.ppermute only.
A program may use at most 64 MiB of HBM per device.

```python
import math
import jax
import jax.numpy as jnp
import numpy as np
from jax import lax

AX = 2
CZ = 256
ASLOT = 32
SWEEPS = 3
ELEMS = 393216
CAP = 256
AGGS = 24576
N_GX = 96
N_GY = 8


def draw_coarse_inverse(key, part):
    key = jax.random.fold_in(key, 11)
    first_key, second_key = jax.random.split(key)
    scales = jnp.exp(jax.random.uniform(first_key, (AGGS,), jnp.float32, math.log(0.5), math.log(2.0)))
    noise = jax.random.normal(second_key, (48, 48, AGGS), jnp.float32)
    identity = jnp.eye(48, dtype=jnp.float32)[:, :, None]
    return scales[None, None, :] * (identity + 0.5 / math.sqrt(48.0) * noise)


def set_ends(drawn, key, low, largest):
    dims = drawn.shape
    spot = [jax.random.randint(jax.random.fold_in(key, axis), (), 0, dims[axis]) for axis in range(len(dims))]
    drawn = drawn.at[tuple(spot)].set(low)
    longest = dims.index(max(dims))
    spot[longest] = (spot[longest] + 1) % dims[longest]
    return drawn.at[tuple(spot)].set(largest)


def shard_levels(own_key, shape, cuts, smallest, top_value):
    def one(dim, parts):
        draws = jax.random.uniform(jax.random.fold_in(jax.random.fold_in(own_key, 6), dim), (parts,), jnp.float32, smallest / len(cuts), top_value / len(cuts))
        return jnp.repeat(jnp.exp(draws), shape[dim] // parts).reshape((-1,) + (1,) * (len(shape) - dim - 1))

    gain = one(*cuts[0])
    for cut in cuts[1:]:
        gain = gain * one(*cut)
    return gain


def deal_out(own_key, own, number, rows, number_of, top, bound, slope):
    sequence = jax.random.permutation(own_key, number_of)
    heavy_load, usual = portions_of(number_of, rows * top, bound, slope, True), portions_of(number_of, rows * top, bound, slope, False)
    places = jnp.arange(number_of)

    def named(lengths, offset_by):
        used = int((lengths > 0).sum())
        fixed = max(1, used // 4)
        passed = fixed + (places - fixed + offset_by * (used - fixed)) % max(1, number_of - fixed)
        return jnp.zeros((number_of,), jnp.int32).at[sequence[jnp.where(places < fixed, places, passed)]].set(jnp.asarray(lengths, jnp.int32))

    lengths = jnp.where(number % 4 == 0, named(heavy_load, number // 4), named(usual, number - number // 4 - 1))
    mixed = jax.random.permutation(jax.random.fold_in(own, 3), number_of)
    source_of, receiver = mixed[0:number_of // 2 * 2:2], mixed[1:number_of // 2 * 2:2]
    margin = jnp.minimum(lengths[source_of] - 1, bound - lengths[receiver]) // 2
    margin = jnp.where((source_of == sequence[0]) | (receiver == sequence[0]) | (lengths[receiver] == 0), 0, jnp.maximum(margin, 0))
    passed = jax.random.randint(jax.random.fold_in(own, 4), (number_of // 2,), 0, 1 << 20) % (margin + 1)
    lengths = lengths.at[source_of].add(-passed).at[receiver].add(passed)
    members = jnp.searchsorted(jnp.cumsum(lengths), jnp.arange(rows * top), side="right").astype(jnp.int32)
    listing = members.reshape(top, rows).T
    listing = listing[jax.random.permutation(jax.random.fold_in(own, 1), rows)]
    offset_by = jax.random.randint(jax.random.fold_in(own, 2), (rows, 1), 0, top)
    return jnp.take_along_axis(listing, (jnp.arange(top)[None, :] + offset_by) % top, axis=1)


def portions_of(number_of, total, most, lean, full):
    portions = [(1 << 20) // math.isqrt(rank ** lean) + 1 for rank in range(1, number_of + 1)]
    largest = most if full else min(most, max(-(-total // number_of), total * portions[0] // sum(portions)))
    least = 1 if total - largest >= number_of - 1 else 0
    counts, rest = [largest] + [least] * (number_of - 1), total - largest - least * (number_of - 1)
    while rest > 0:
        candidates = [i for i in range(1, number_of) if counts[i] < largest] or [i for i in range(1, number_of) if counts[i] < most]
        whole, left = sum([portions[i] for i in candidates]), rest
        for i in candidates:
            extra = min(most - counts[i], max(1, left * portions[i] // whole), rest)
            counts[i] = counts[i] + extra
            rest = rest - extra
    return np.array(counts)


def bell_draw(own_key, shape, spread, limit, cuts=(), kind=jnp.bfloat16):
    result = spread * jax.random.normal(own_key, shape, jnp.float32)
    if cuts:
        result = result * shard_levels(own_key, shape, cuts, -0.22, 0.18)
    return jnp.clip(result, -limit, limit).astype(kind)


def setup_inputs(seed: int = 0) -> dict:
    arg_keys = jax.random.split(jax.random.key(seed), 15)
    state = bell_draw(arg_keys[0], (6, 125, ELEMS), 1.0, 6.0, ((2, 768),))
    forcing = bell_draw(arg_keys[1], (6, 125, ELEMS), 1.0, 6.0, ((2, 768),))
    volume_flux_matrix = bell_draw(arg_keys[2], (125, 125), 125 ** -0.5, 0.5)
    viscous_matrix = bell_draw(arg_keys[3], (125, 125), 125 ** -0.5, 0.5)
    linear_flux_matrix = bell_draw(arg_keys[4], (6, 6), 6 ** -0.5, 2.5, (), jnp.float32)
    viscosity = jnp.clip(jnp.exp(math.log(1.0) - 2.3025851 * jax.random.uniform(arg_keys[5], (ELEMS,), jnp.float32) ** shard_levels(arg_keys[5], (ELEMS,), ((0, 768),), -0.2, 0.2)), 0.1, 1.0)
    lift = bell_draw(arg_keys[6], (6, 125, 25), 150 ** -0.5, 0.5)
    wall_flags = set_ends((jax.random.randint(arg_keys[7], (ELEMS,), 0, 4) < 1).astype(jnp.int32), jax.random.fold_in(arg_keys[7], 1), 0, 1)
    restriction_weight = bell_draw(arg_keys[8], (8, 125), 1000 ** -0.5, 0.1875, (), jnp.float32)
    owner_keys = jax.random.split(jax.random.fold_in(arg_keys[9], 1), ELEMS // (AX * CZ))
    owner_turns = jax.random.permutation(jax.random.fold_in(arg_keys[9], 3), ELEMS // (AX * CZ))
    owner = jax.vmap(lambda own, number: deal_out(jax.random.fold_in(arg_keys[9], 2), own, number, AX * CZ, N_GY, 1, CAP, 2))(owner_keys, owner_turns).reshape((ELEMS, 1))
    slot = set_ends(jax.random.randint(arg_keys[10], (ELEMS,), 0, ASLOT), jax.random.fold_in(arg_keys[10], 1), 0, ASLOT - 1).astype(jnp.int32)
    coarse_inverse = draw_coarse_inverse(jax.random.fold_in(arg_keys[14], 71), 0)
    coupling = bell_draw(arg_keys[12], (48, 48), 192 ** -0.5, 0.4375, (), jnp.float32)
    prolongation_weight = bell_draw(arg_keys[13], (125, 8), 8 ** -0.5, 2.0, (), jnp.float32)
    return {"state": state, "forcing": forcing, "volume_flux_matrix": volume_flux_matrix, "viscous_matrix": viscous_matrix, "linear_flux_matrix": linear_flux_matrix, "viscosity": viscosity, "lift": lift, "wall_flags": wall_flags, "restriction_weight": restriction_weight, "owner": owner, "slot": slot, "coarse_inverse": coarse_inverse, "coupling": coupling, "prolongation_weight": prolongation_weight}


relaxation = 0.7
wall_rate = 2.0
finest_level = lax.Precision.HIGHEST


def to_grid(trace_vals):
    shaped = trace_vals.reshape(6, 25, N_GX, N_GY, AX, CZ)
    return shaped.transpose(0, 1, 2, 4, 3, 5).reshape(6, 25, N_GX * AX, N_GY, CZ)


def from_grid(grid_vals):
    shaped = grid_vals.reshape(6, 25, N_GX, AX, N_GY, CZ)
    return shaped.transpose(0, 1, 2, 4, 3, 5).reshape(6, 25, N_GX * N_GY * AX * CZ)


def reference(state, forcing, volume_flux_matrix, viscous_matrix, linear_flux_matrix, viscosity, lift, wall_flags, restriction_weight, owner, slot, coarse_inverse, coupling, prolongation_weight):
    element_rows = state.shape[2]
    widened_values = state.astype(jnp.float32)
    nodal_vals = widened_values.reshape(6, 5, 5, 5, element_rows)
    owned = [nodal_vals[:, 0], nodal_vals[:, 4], nodal_vals[:, :, 0], nodal_vals[:, :, 4], nodal_vals[:, :, :, 0], nodal_vals[:, :, :, 4]]
    owned = [to_grid(face_nodes.reshape(6, 25, element_rows)) for face_nodes in owned]
    blanks = jnp.zeros_like(owned[0][..., :1])
    nearby = [jnp.roll(owned[1], 1, 2), jnp.roll(owned[0], -1, 2), jnp.roll(owned[3], 1, 3), jnp.roll(owned[2], -1, 3),
              jnp.concatenate([blanks, owned[5][..., :-1]], 4), jnp.concatenate([owned[4][..., 1:], blanks], 4)]
    interface_jumps = jnp.stack([from_grid(nearby[face_no] - owned[face_no]) for face_no in range(6)]).astype(jnp.bfloat16)
    lifted_values = jnp.einsum('poc,pbcj->boj', lift.astype(jnp.float32), interface_jumps.astype(jnp.float32), precision=finest_level)
    stiffness_matrix = jnp.einsum('sz,izy->isy', volume_flux_matrix.astype(jnp.float32), widened_values, precision=finest_level)
    flux_contribution = jnp.einsum('qk,kgs->qgs', linear_flux_matrix, stiffness_matrix, precision=finest_level)
    viscous_update = jnp.einsum('sz,izy->isy', viscous_matrix.astype(jnp.float32), widened_values, precision=finest_level)
    marker = (jnp.arange(6) == 5).astype(jnp.float32)[:, None, None]
    wall_term = wall_rate * marker * wall_flags.astype(jnp.float32)[None, None, :] * widened_values
    complete_residual = forcing.astype(jnp.float32) - flux_contribution - viscosity[None, None, :] * viscous_update - wall_term + lifted_values
    restricted_values = jnp.einsum('wo,xoi->xwi', restriction_weight, complete_residual, precision=finest_level).reshape(48, element_rows)
    device_rank = jnp.arange(element_rows, dtype=jnp.int32) // (AX * CZ)
    agg_index = ((device_rank // N_GY) * N_GY + owner[:, 0]) * ASLOT + slot
    totals = jax.ops.segment_sum(restricted_values.T, agg_index, num_segments=AGGS).T
    coarse = jnp.zeros((48, AGGS), jnp.float32)
    for sweep_no in range(SWEEPS):
        loop_view = coarse.reshape(48, N_GX, N_GY * ASLOT)
        beside_all = (jnp.roll(loop_view, 1, 1) + jnp.roll(loop_view, -1, 1)).reshape(48, AGGS)
        source = totals - jnp.dot(coupling, beside_all, precision=finest_level)
        coarse = (1.0 - relaxation) * coarse + relaxation * jnp.einsum('ija,ja->ia', coarse_inverse, source, precision=finest_level)
    chosen_rows = coarse[:, agg_index].reshape(6, 8, element_rows)
    correction = jnp.einsum('az,tzl->tal', prolongation_weight, chosen_rows, precision=finest_level)
    return complete_residual.astype(jnp.bfloat16), correction.astype(jnp.bfloat16)
```

```python
import jax
import jax.numpy as jnp
import numpy as np
from jax import lax
from jax.experimental import pallas as pl
from jax.experimental.pallas import tpu as pltpu
from jax.sharding import PartitionSpec as P

NV = 6
NN = 125
NF = 25
FR = 32
ASLOT = 32
MEMBERS = 8
RELAX = 0.7
WALL = 2.0
BF = jnp.bfloat16
F32 = jnp.float32
TOP = lax.Precision.HIGHEST
VMEM = pl.BlockSpec(memory_space=pltpu.VMEM)
SMEM = pl.BlockSpec(memory_space=pltpu.SMEM)


def face_nodes(face):
    p, q, r = np.meshgrid(np.arange(5), np.arange(5), np.arange(5), indexing="ij")
    axis, end = (p, q, r)[face // 2], 4 * (face % 2)
    return ((p * 5 + q) * 5 + r)[axis == end]


def picker(faces):
    rows = np.zeros((FR * len(faces), NN), np.float32)
    for k, face in enumerate(faces):
        rows[FR * k + np.arange(NF), face_nodes(face)] = 1.0
    return rows


def dot(a, b, **kw):
    return jnp.dot(a, b, preferred_element_type=F32, **kw)


def split(x):
    high = x.astype(BF)
    return high, (x - high.astype(F32)).astype(BF)


def call(kernel, outs, *args, scratch=(), smem=(), flops=10**8, nbytes=10**6):
    return pl.pallas_call(
        kernel,
        out_shape=outs,
        in_specs=[SMEM if i in smem else VMEM for i in range(len(args))],
        out_specs=jax.tree.map(lambda _: VMEM, outs),
        scratch_shapes=list(scratch),
        compiler_params=pltpu.CompilerParams(vmem_limit_bytes=40 * 2**20),
        cost_estimate=pl.CostEstimate(flops=flops, bytes_accessed=nbytes, transcendentals=0),
    )(*args)


def faces_kernel(state, pick, low_x, high_x, low_y, high_y):
    half = state.shape[2] // 2
    for v in range(NV):
        found = dot(pick[...], state[v]).astype(BF)
        low_x[v] = found[:FR, :half]
        high_x[v] = found[FR : 2 * FR, half:]
        low_y[v] = found[2 * FR : 3 * FR]
        high_y[v] = found[3 * FR :]


def prepare_kernel(inverse, lift_t, restrict, grid_inverse, lift_near, lift_far, r_parts, rl_parts):
    lanes = grid_inverse.shape[2]
    rows = inverse.shape[0] // 3
    modes = inverse.shape[2]
    blank = jnp.zeros((lanes - 3 * ASLOT, modes), F32)
    for r in range(rows):
        stacked = jnp.concatenate([inverse[r], inverse[rows + r], inverse[2 * rows + r], blank], axis=0)
        grid_inverse[r] = RELAX * stacked.T
    r_high, r_low = split(restrict[...])
    r_parts[...] = jnp.concatenate([r_high, r_low], axis=0)
    gap = jnp.zeros((FR - NF, NN), F32)
    lifts = [jnp.concatenate([lift_t[f].astype(F32), gap], axis=0).T for f in range(6)]
    for a in range(2):
        lift_near[a] = jnp.concatenate([lifts[1 - a], lifts[4], lifts[5]], axis=1).astype(BF)
        far = jnp.concatenate([lifts[a], lifts[2], lifts[3]], axis=1)
        lift_far[a] = far.astype(BF)
        high, low = split(dot(restrict[...], far, precision=TOP))
        rl_parts[a] = jnp.concatenate([high, low], axis=0)


def volume_kernel(
    mix, state, forcing, volume, viscous, viscosity, flags, pick, lift_near, r_parts, partial, restricted, flux
):
    half = state.shape[2] // 2
    lanes = state.shape[2]
    place = lax.broadcasted_iota(jnp.int32, (FR, lanes), 1) % half
    first, last = place == 0, place == half - 1
    visc = viscosity[...]
    for v in range(NV):
        own = state[v]
        flux[v] = dot(volume[...], own)
        traces = dot(pick[...], own)
        t0, t1, t4, t5 = (traces[FR * k : FR * (k + 1)] for k in range(4))
        below = jnp.where(first, 0.0, pltpu.roll(t5, 1, 1))
        above = jnp.where(last, 0.0, pltpu.roll(t4, lanes - 1, 1))
        j4 = below - t4
        j5 = above - t5
        across = t0[:, half:] - t1[:, :half]
        parts = []
        for a in range(2):
            cut = slice(a * half, (a + 1) * half)
            jumps = jnp.concatenate([across if a == 0 else -across, j4[:, cut], j5[:, cut]], axis=0)
            parts.append(dot(lift_near[a], jumps.astype(BF)))
        lifted = jnp.concatenate(parts, axis=1)
        local = forcing[v].astype(F32) - visc * dot(viscous[...], own) + lifted
        if v == NV - 1:
            local = local - (WALL * flags[...].astype(F32)) * own.astype(F32)
        partial[v] = local
    for low in range(0, NN, 8):
        rows = slice(low, min(low + 8, NN))
        pieces = [flux[k, rows] for k in range(NV)]
        for q in range(NV):
            total = mix[q, 0] * pieces[0]
            for k in range(1, NV):
                total = total + mix[q, k] * pieces[k]
            partial[q, rows] = partial[q, rows] - total
    for v in range(NV):
        high, low = split(partial[v])
        both = dot(r_parts[...], high)
        restricted[8 * v : 8 * v + 8] = both[:8] + both[8:] + dot(r_parts[:8], low)


def far_jumps(v, a, half, near, own):
    cut = slice(a * half, (a + 1) * half)
    nx, ny_low, ny_high = near[a][v], near[2][v][:, cut], near[3][v][:, cut]
    ox, oy_low, oy_high = own[a][v], own[2][v][:, cut], own[3][v][:, cut]
    pairs = ((nx, ox), (ny_low, oy_low), (ny_high, oy_high))
    return jnp.concatenate([n.astype(F32) - o.astype(F32) for n, o in pairs], axis=0).astype(BF)


def keys_of(owner, slot):
    return owner[...] * ASLOT + slot[...]


def one_hot(keys):
    groups = MEMBERS * ASLOT
    return (lax.broadcasted_iota(jnp.int32, (groups, keys.shape[1]), 0) == keys).astype(F32).astype(BF)


def sums_kernel(n0, n1, n2, n3, o0, o1, o2, o3, rl_parts, restricted, owner, slot, blocks):
    near, own = (n0, n1, n2, n3), (o0, o1, o2, o3)
    half = owner.shape[1] // 2
    highs, lows = [], []
    for v in range(NV):
        parts = []
        for a in range(2):
            both = dot(rl_parts[a], far_jumps(v, a, half, near, own))
            parts.append(both[:8] + both[8:])
        high, low = split(restricted[8 * v : 8 * v + 8] + jnp.concatenate(parts, axis=1))
        highs.append(high.astype(F32))
        lows.append(low.astype(F32))
    stacked = jnp.concatenate(highs + lows, axis=0).astype(BF)
    spread = one_hot(keys_of(owner, slot))
    both = lax.dot_general(stacked, spread, (((1,), (1,)), ((), ())), preferred_element_type=F32)
    sums = both[: 8 * NV] + both[8 * NV :]
    group = lax.broadcasted_iota(jnp.int32, (16, 128), 1) // ASLOT
    for m in range(MEMBERS):
        block = jnp.zeros((16, 128), F32)
        for k in range(3):
            piece = sums[16 * k : 16 * k + 16, (m // 4) * 128 : (m // 4 + 1) * 128]
            turn = ((k - m % 4) * ASLOT) % 128
            piece = pltpu.roll(piece, turn, 1) if turn else piece
            block = jnp.where(group == k, piece, block)
        blocks[m] = block


def residual_kernel(n0, n1, n2, n3, o0, o1, o2, o3, lift_far, partial, residual):
    near, own = (n0, n1, n2, n3), (o0, o1, o2, o3)
    half = partial.shape[2] // 2
    for v in range(NV):
        for a in range(2):
            cut = slice(a * half, (a + 1) * half)
            lifted = dot(lift_far[a], far_jumps(v, a, half, near, own))
            residual[v, :, cut] = (partial[v, :, cut] + lifted).astype(BF)


def opened(packed):
    group = lax.broadcasted_iota(jnp.int32, (16, 128), 1) // ASLOT
    rows = []
    for k in range(3):
        only = jnp.where(group == k, packed, 0.0)
        two = only + pltpu.roll(only, 32, 1)
        rows.append(two + pltpu.roll(two, 64, 1))
    return jnp.concatenate(rows, axis=0)


def solve(grid_inverse, source, out):
    for r in range(16):
        out[r : r + 1] = jnp.sum(grid_inverse[r] * source, axis=0, keepdims=True)


def first_kernel(blocks, grid_inverse, totals, coarse):
    packed = jnp.sum(blocks[...], axis=0)
    source = opened(packed)
    totals[...] = source
    solve(grid_inverse, source, coarse)


def sweep_kernel(up, down, totals, coupling, before, grid_inverse, coarse):
    beside = opened(up[...] + down[...])
    source = totals[...] - dot(coupling[...], beside, precision=TOP)
    solve(grid_inverse, source, coarse)
    coarse[...] = (1.0 - RELAX) * before[...] + coarse[...]


def last_sweep_kernel(up, down, totals, coupling, before, grid_inverse, blocks, scratch):
    sweep_kernel(up, down, totals, coupling, before, grid_inverse, scratch)
    for m in range(MEMBERS):
        blocks[m] = scratch[...]


def correction_kernel(blocks, prolong_t, owner, slot, correction):
    weights = prolong_t[...].T
    select = one_hot(keys_of(owner, slot))
    group = lax.broadcasted_iota(jnp.int32, (8, 128), 1) // ASLOT
    for v in range(NV):
        k, rows = v // 2, slice(8 * (v % 2), 8 * (v % 2) + 8)
        halves = []
        for h in range(MEMBERS // 4):
            value = jnp.zeros((8, 128), F32)
            for w in range(4):
                turn = ((w - k) * ASLOT) % 128
                piece = blocks[4 * h + w, rows]
                piece = pltpu.roll(piece, turn, 1) if turn else piece
                value = jnp.where(group == w, piece, value)
            halves.append(value)
        wide = dot(weights, jnp.concatenate(halves, axis=1), precision=TOP).astype(BF)
        correction[v] = dot(wide, select).astype(BF)


def shifted(value, axis, by):
    size = lax.axis_size(axis)
    return lax.ppermute(value, axis, [(i, (i + by) % size) for i in range(size)])


def struct(shape, dtype):
    return jax.ShapeDtypeStruct(shape, dtype)


def per_device(
    state,
    forcing,
    volume_flux_matrix,
    viscous_matrix,
    linear_flux_matrix,
    viscosity,
    lift,
    wall_flags,
    restriction_weight,
    owner,
    slot,
    coarse_inverse,
    coupling,
    prolongation_weight,
):
    elems = state.shape[2]
    half = elems // 2
    owner, slot = owner.reshape(1, elems), slot.reshape(1, elems)
    viscosity, flags = viscosity.reshape(1, elems), wall_flags.reshape(1, elems)
    pick_far = jnp.asarray(picker((0, 1, 2, 3)), BF)
    pick_near = jnp.asarray(picker((0, 1, 4, 5)), BF)
    x_face, y_face = struct((NV, FR, half), BF), struct((NV, FR, elems), BF)
    own = call(faces_kernel, (x_face, x_face, y_face, y_face), state, pick_far)
    near = (
        shifted(own[1], "gx", 1),
        shifted(own[0], "gx", -1),
        shifted(own[3], "gy", 1),
        shifted(own[2], "gy", -1),
    )
    inverse, lift_t, _ = lax.optimization_barrier(
        (jnp.transpose(coarse_inverse, (0, 2, 1)), jnp.transpose(lift, (0, 2, 1)), own[0])
    )
    grid_inverse, lift_near, lift_far, r_parts, rl_parts = call(
        prepare_kernel,
        (
            struct((16, 48, 128), F32),
            struct((2, NN, 3 * FR), BF),
            struct((2, NN, 3 * FR), BF),
            struct((16, NN), BF),
            struct((2, 16, 3 * FR), BF),
        ),
        inverse,
        lift_t,
        restriction_weight,
    )
    partial, restricted = call(
        volume_kernel,
        (struct((NV, NN, elems), F32), struct((48, elems), F32)),
        linear_flux_matrix,
        state,
        forcing,
        volume_flux_matrix,
        viscous_matrix,
        viscosity,
        flags,
        pick_near,
        lift_near,
        r_parts,
        scratch=[pltpu.VMEM((NV, NN, elems), F32)],
        smem=(0,),
        flops=10**9,
        nbytes=4 * 10**6,
    )
    blocks = call(
        sums_kernel, struct((MEMBERS, 16, 128), F32), *near, *own, rl_parts, restricted, owner, slot
    )
    blocks = lax.all_to_all(blocks, "gy", 0, 0, tiled=True)
    totals, coarse = call(
        first_kernel, (struct((48, 128), F32), struct((16, 128), F32)), blocks, grid_inverse
    )
    partial, _ = lax.optimization_barrier((partial, coarse))
    up, down = shifted(coarse, "gx", 1), shifted(coarse, "gx", -1)
    residual = call(
        residual_kernel, struct((NV, NN, elems), BF), *near, *own, lift_far, partial,
        flops=10**9, nbytes=4 * 10**6,
    )
    coarse = call(
        sweep_kernel, struct((16, 128), F32), up, down, totals, coupling, coarse, grid_inverse
    )
    up, down = shifted(coarse, "gx", 1), shifted(coarse, "gx", -1)
    blocks = call(
        last_sweep_kernel,
        struct((MEMBERS, 16, 128), F32),
        up,
        down,
        totals,
        coupling,
        coarse,
        grid_inverse,
        scratch=[pltpu.VMEM((16, 128), F32)],
    )
    blocks = lax.all_to_all(blocks, "gy", 0, 0, tiled=True)
    correction = call(
        correction_kernel,
        struct((NV, NN, elems), BF),
        blocks,
        jnp.transpose(prolongation_weight),
        owner,
        slot,
    )
    return residual, correction


def solution(mesh):
    split_last = P(None, None, ("gx", "gy"))
    flat = P(("gx", "gy"))
    return jax.shard_map(
        per_device,
        mesh=mesh,
        in_specs=(
            split_last,
            split_last,
            P(),
            P(),
            P(),
            flat,
            P(),
            flat,
            P(),
            P(("gx", "gy"), None),
            flat,
            split_last,
            P(),
            P(),
        ),
        out_specs=(split_last, split_last),
        check_vma=False,
    )
```

```python
import jax
import jax.numpy as jnp
from jax import lax
from jax.experimental import pallas as pl
from jax.experimental.pallas import tpu as pltpu
from jax.sharding import PartitionSpec as P

NV = 6
NN = 125
NF = 25
FR = 32
ASLOT = 32
MEMBERS = 8
RELAX = 0.7
WALL = 2.0
BF = jnp.bfloat16
F32 = jnp.float32
TOP = lax.Precision.HIGHEST
VMEM = pl.BlockSpec(memory_space=pltpu.VMEM)
ANY = pl.BlockSpec(memory_space=pl.ANY)
HBM = pl.BlockSpec(memory_space=pltpu.HBM)
SMEM = pl.BlockSpec(memory_space=pltpu.SMEM)


def picker(faces, columns=NN):
    place = lax.broadcasted_iota(jnp.int32, (FR, columns), 0)
    node = lax.broadcasted_iota(jnp.int32, (FR, columns), 1)
    p, line = (node * 41) >> 10, (node * 205) >> 10
    q, r = line - 5 * p, node - 5 * line
    rows = []
    for face in faces:
        end = 4 * (face % 2)
        held, index = ((p, 5 * q + r), (q, 5 * p + r), (r, 5 * p + q))[face // 2]
        rows.append(((held == end) & (index == place) & (place < NF)).astype(F32))
    return jnp.concatenate(rows, axis=0).astype(BF)


def dot(a, b, **kw):
    return jnp.dot(a, b, preferred_element_type=F32, **kw)


def split(x):
    high = x.astype(BF)
    return high, (x - high.astype(F32)).astype(BF)


def call(kernel, outs, *args, scratch=(), smem=(), loose=(), hbm_out=(), flops=1000, nbytes=1000):
    flat, tree = jax.tree.flatten(outs)
    return pl.pallas_call(
        kernel,
        out_shape=outs,
        in_specs=[SMEM if i in smem else ANY if i in loose else VMEM for i in range(len(args))],
        out_specs=jax.tree.unflatten(tree, [HBM if i in hbm_out else VMEM for i in range(len(flat))]),
        scratch_shapes=list(scratch),
        compiler_params=pltpu.CompilerParams(vmem_limit_bytes=24 * 2**20),
        cost_estimate=pl.CostEstimate(flops=flops, bytes_accessed=nbytes, transcendentals=0),
    )(*args)


def is_odd():
    return lax.axis_index("gx") % 2 == 1


def faces_kernel(state, low_y, high_y, near_x, far_x):
    half = state.shape[2] // 2
    pick = picker((0, 1, 2, 3))
    odd = is_odd()
    for v in range(NV):
        found = dot(pick, state[v])
        low, high = found[:FR, :half], found[FR : 2 * FR, half:]
        far_x[v] = jnp.where(odd, high, low).astype(BF)
        near_x[v] = jnp.where(odd, low, high).astype(BF)
        low_y[v] = found[2 * FR : 3 * FR].astype(BF)
        high_y[v] = found[3 * FR :].astype(BF)


def halves(x):
    return [part.astype(F32) for part in split(x)]


def transposed_lifts(lift_t):
    gap = jnp.zeros((FR - NF, NN), F32)
    lifts = [jnp.concatenate([lift_t[f].astype(F32), gap], axis=0).T for f in range(6)]
    return jnp.concatenate(lifts, axis=1).astype(BF)


def weights_kernel(volume, viscous, lift_t, restrict, state_side, forcing_side, lift_side):
    both = jnp.concatenate(halves(restrict[...]), axis=0).astype(BF)

    def restricted(matrix):
        parts = dot(both, matrix)
        return halves(parts[:8] + parts[8:])

    lift_side[...] = jnp.concatenate(restricted(transposed_lifts(lift_t)), axis=0).astype(BF)
    forcing_side[...] = both
    parts = restricted(volume[...]) + restricted(viscous[...]) + halves(restrict[...])
    state_side[...] = jnp.concatenate([picker((0, 1, 4, 5)).astype(F32), *parts], axis=0).astype(BF)


def inverse_kernel(inverse, coupling, coarse_side):
    lanes = coarse_side.shape[2]
    rows, modes = inverse.shape[0] // 3, inverse.shape[2]
    blank = jnp.zeros((lanes - 3 * ASLOT, modes), F32)
    for r in range(rows):
        stacked = jnp.concatenate([inverse[r], inverse[rows + r], inverse[2 * rows + r], blank], axis=0)
        coarse_side[r] = RELAX * stacked.T
    coarse_side[rows] = jnp.concatenate([coupling[...], jnp.zeros((modes, lanes - modes), F32)], axis=1)


def restricted_kernel(mix, forcing, state, viscosity, flags, state_side, forcing_side, near, restricted):
    lanes = state.shape[2]
    half = lanes // 2
    place = lax.broadcasted_iota(jnp.int32, (FR, lanes), 1) % half
    visc = viscosity[...]
    fluxes, local = [], []
    for v in range(NV):
        found = dot(state_side[...], state[v])
        given = dot(forcing_side[...], forcing[v])
        t0, t1, t4, t5 = (found[FR * k : FR * (k + 1)] for k in range(4))
        across = t0[:, half:] - t1[:, :half]
        below = jnp.where(place == 0, 0.0, pltpu.roll(t5, 1, 1))
        above = jnp.where(place == half - 1, 0.0, pltpu.roll(t4, lanes - 1, 1))
        near[v, :FR] = jnp.concatenate([across, -across], axis=1).astype(BF)
        near[v, FR : 2 * FR] = (below - t4).astype(BF)
        near[v, 2 * FR :] = (above - t5).astype(BF)
        first = 4 * FR
        rows = [found[first + 16 * k : first + 16 * k + 8] + found[first + 16 * k + 8 : first + 16 * k + 16] for k in range(3)]
        total = given[:8] + given[8:] - visc * rows[1]
        if v == NV - 1:
            total = total - (WALL * flags[...].astype(F32)) * rows[2]
        fluxes.append(rows[0])
        local.append(total)
    for q in range(NV):
        total = local[q]
        for k in range(NV):
            total = total - mix[q, k] * fluxes[k]
        restricted[8 * q : 8 * q + 8] = total


def products_kernel(mix, forcing, state, volume, viscous, viscosity, flags, partial, flux):
    for v in range(NV):
        u = state[v]
        flux[v, :NN] = dot(volume[...], u)
        total = forcing[v].astype(F32) - viscosity[...] * dot(viscous[...], u)
        if v == NV - 1:
            total = total - (WALL * flags[...].astype(F32)) * u.astype(F32)
        partial[v] = total
    for q in range(NV):
        for low in range(0, NN, 16):
            rows = slice(low, min(low + 16, NN))
            total = partial[q, rows]
            for k in range(NV):
                total = total - mix[q, k] * flux[k, rows]
            partial[q, rows] = total


def residual_kernel(partial, jumps, lift_t, residual, out, sems):
    lifts = transposed_lifts(lift_t)
    sends = []
    for v in range(NV):
        out[v] = (partial[v] + dot(lifts, jumps[v])).astype(BF)
        sends.append(pltpu.make_async_copy(out.at[v], residual.at[v], sems.at[v]))
        sends[-1].start()
    for copy in sends:
        copy.wait()


def keys_of(owner, slot):
    return owner[...] * ASLOT + slot[...]


def one_hot(keys):
    groups = MEMBERS * ASLOT
    return (lax.broadcasted_iota(jnp.int32, (groups, keys.shape[1]), 0) == keys).astype(F32).astype(BF)


def sums_kernel(n1, n0, n2, n3, o2, o3, o1, o0, near, lift_side, restricted, owner, slot, blocks, jumps):
    half = owner.shape[1] // 2

    odd = is_odd()

    def difference(a, b):
        return a.astype(F32) - b.astype(F32)

    highs, lows = [], []
    for v in range(NV):
        far, close = difference(n0[v], o0[v]), difference(n1[v], o1[v])
        jumps[v, :FR, :half] = jnp.where(odd, close, far).astype(BF)
        jumps[v, :FR, half:] = near[v, :FR, half:]
        jumps[v, FR : 2 * FR, :half] = near[v, :FR, :half]
        jumps[v, FR : 2 * FR, half:] = jnp.where(odd, far, close).astype(BF)
        jumps[v, 2 * FR : 3 * FR] = difference(n2[v], o2[v]).astype(BF)
        jumps[v, 3 * FR : 4 * FR] = difference(n3[v], o3[v]).astype(BF)
        jumps[v, 4 * FR :] = near[v, FR:]
        both = dot(lift_side[...], jumps[v])
        high, low = halves(restricted[8 * v : 8 * v + 8] + both[:8] + both[8:])
        highs.append(high)
        lows.append(low)
    stacked = jnp.concatenate(highs + lows, axis=0).astype(BF)
    spread = one_hot(keys_of(owner, slot))
    both = lax.dot_general(stacked, spread, (((1,), (1,)), ((), ())), preferred_element_type=F32)
    sums = both[: 8 * NV] + both[8 * NV :]
    group = lax.broadcasted_iota(jnp.int32, (16, 128), 1) // ASLOT
    for m in range(MEMBERS):
        block = jnp.zeros((16, 128), F32)
        for k in range(3):
            piece = sums[16 * k : 16 * k + 16, (m // 4) * 128 : (m // 4 + 1) * 128]
            turn = ((k - m % 4) * ASLOT) % 128
            piece = pltpu.roll(piece, turn, 1) if turn else piece
            block = jnp.where(group == k, piece, block)
        blocks[m] = block


def opened(packed):
    group = lax.broadcasted_iota(jnp.int32, (16, 128), 1) // ASLOT
    rows = []
    for k in range(3):
        only = jnp.where(group == k, packed, 0.0)
        two = only + pltpu.roll(only, 32, 1)
        rows.append(two + pltpu.roll(two, 64, 1))
    return jnp.concatenate(rows, axis=0)


def solve(coarse_side, source, out):
    for r in range(16):
        out[r : r + 1] = jnp.sum(coarse_side[r] * source, axis=0, keepdims=True)


def first_kernel(blocks, coarse_side, _, totals, coarse):
    packed = jnp.sum(blocks[...], axis=0)
    source = opened(packed)
    totals[...] = source
    solve(coarse_side, source, coarse)


def sweep_kernel(up, down, totals, before, coarse_side, coarse):
    beside = opened(up[...] + down[...])
    coupling = coarse_side[16][:, : beside.shape[0]]
    source = totals[...] - dot(coupling, beside, precision=TOP)
    solve(coarse_side, source, coarse)
    coarse[...] = (1.0 - RELAX) * before[...] + coarse[...]


def last_sweep_kernel(up, down, totals, before, coarse_side, blocks, scratch):
    sweep_kernel(up, down, totals, before, coarse_side, scratch)
    for m in range(MEMBERS):
        blocks[m] = scratch[...]


def correction_kernel(blocks, prolong_t, owner, slot, correction, wide, out, sems):
    high, low = (x.astype(F32) for x in split(prolong_t[...]))
    weights = jnp.concatenate([high, low, high], axis=0)
    gap = jnp.zeros((weights.shape[0], wide.shape[0] // NV - NN), F32)
    weights = jnp.concatenate([weights, gap], axis=1).T.astype(BF)
    select = one_hot(keys_of(owner, slot))
    group = lax.broadcasted_iota(jnp.int32, (8, 128), 1) // ASLOT
    step = wide.shape[0] // NV
    for v in range(NV):
        k, rows = v // 2, slice(8 * (v % 2), 8 * (v % 2) + 8)
        parts = []
        for h in range(MEMBERS // 4):
            value = jnp.zeros((8, 128), F32)
            for w in range(4):
                turn = ((w - k) * ASLOT) % 128
                piece = blocks[4 * h + w, rows]
                piece = pltpu.roll(piece, turn, 1) if turn else piece
                value = jnp.where(group == w, piece, value)
            parts.append(value)
        high, low = (x.astype(F32) for x in split(jnp.concatenate(parts, axis=1)))
        values = jnp.concatenate([high, high, low], axis=0).astype(BF)
        wide[step * v : step * (v + 1)] = dot(weights, values).astype(BF)
    sends = []
    for first in range(0, NV, 2):
        found = dot(wide[step * first : step * (first + 2)], select)
        for v in (first, first + 1):
            out[v] = found[step * (v - first) : step * (v - first) + NN].astype(BF)
            sends.append(pltpu.make_async_copy(out.at[v], correction.at[v], sems.at[v]))
            sends[-1].start()
    for copy in sends:
        copy.wait()


def shifted(value, axis, by):
    size = lax.axis_size(axis)
    return lax.ppermute(value, axis, [(i, (i + by) % size) for i in range(size)])


def swapped(value, start):
    size = lax.axis_size("gx")
    return lax.ppermute(value, "gx", [(i, (i + (1 if i % 2 == start else -1)) % size) for i in range(size)])


def struct(shape, dtype):
    return jax.ShapeDtypeStruct(shape, dtype)


def per_device(
    state,
    forcing,
    volume_flux_matrix,
    viscous_matrix,
    linear_flux_matrix,
    viscosity,
    lift,
    wall_flags,
    restriction_weight,
    owner,
    slot,
    coarse_inverse,
    coupling,
    prolongation_weight,
):
    elems = state.shape[2]
    half = elems // 2
    owner, slot = owner.reshape(1, elems), slot.reshape(1, elems)
    viscosity, flags = viscosity.reshape(1, elems), wall_flags.reshape(1, elems)
    x_face, y_face = struct((NV, FR, half), BF), struct((NV, FR, elems), BF)
    field = struct((NV, NN, elems), BF)
    own = call(faces_kernel, (y_face, y_face, x_face, x_face), state, flops=2 * 10**10)
    far_x, near_x = swapped(own[3], 1), swapped(own[2], 0)
    restrict, inverse, _ = lax.optimization_barrier(
        (restriction_weight, jnp.transpose(coarse_inverse, (0, 2, 1)), own[0])
    )
    coarse_side = call(inverse_kernel, struct((17, 48, 128), F32), inverse, coupling)
    near = (near_x, far_x, shifted(own[1], "gy", 1), shifted(own[0], "gy", -1))
    lift_t = jnp.transpose(lift, (0, 2, 1))
    state_side, forcing_side, lift_side = call(
        weights_kernel,
        (struct((4 * FR + 48, NN), BF), struct((16, NN), BF), struct((16, 6 * FR), BF)),
        volume_flux_matrix,
        viscous_matrix,
        lift_t,
        restrict,
    )
    inner, restricted = call(
        restricted_kernel,
        (struct((NV, 3 * FR, elems), BF), struct((48, elems), F32)),
        linear_flux_matrix,
        forcing,
        state,
        viscosity,
        flags,
        state_side,
        forcing_side,
        smem=(0,),
    )
    restricted, coarse_side = lax.optimization_barrier((restricted, coarse_side))
    blocks, jumps = call(
        sums_kernel,
        (struct((MEMBERS, 16, 128), F32), struct((NV, 6 * FR, elems), BF)),
        *near,
        *own,
        inner,
        lift_side,
        restricted,
        owner,
        slot,
    )
    viscous_matrix, _ = lax.optimization_barrier((viscous_matrix, blocks))
    partial = call(
        products_kernel,
        struct((NV, NN, elems), F32),
        linear_flux_matrix,
        forcing,
        state,
        volume_flux_matrix,
        viscous_matrix,
        viscosity,
        flags,
        scratch=[pltpu.VMEM((NV, 128, elems), F32)],
        smem=(0,),
    )
    blocks = lax.all_to_all(blocks, "gy", 0, 0, tiled=True)
    totals, coarse = call(
        first_kernel,
        (struct((48, 128), F32), struct((16, 128), F32)),
        blocks,
        coarse_side,
        partial,
        loose=(2,),
    )
    up, down = swapped(coarse, 0), swapped(coarse, 1)
    coarse = call(sweep_kernel, struct((16, 128), F32), up, down, totals, coarse, coarse_side)
    up, down = swapped(coarse, 0), swapped(coarse, 1)
    blocks = call(
        last_sweep_kernel,
        struct((MEMBERS, 16, 128), F32),
        up,
        down,
        totals,
        coarse,
        coarse_side,
        scratch=[pltpu.VMEM((16, 128), F32)],
    )
    partial, _ = lax.optimization_barrier((partial, blocks))
    residual = call(
        residual_kernel,
        field,
        partial,
        jumps,
        lift_t,
        hbm_out=(0,),
        scratch=[pltpu.VMEM((NV, NN, elems), BF), pltpu.SemaphoreType.DMA((NV,))],
    )
    blocks = lax.all_to_all(blocks, "gy", 0, 0, tiled=True)
    correction = call(
        correction_kernel,
        field,
        blocks,
        jnp.transpose(prolongation_weight),
        owner,
        slot,
        hbm_out=(0,),
        scratch=[
            pltpu.VMEM((128 * NV, MEMBERS * ASLOT), BF),
            pltpu.VMEM((NV, NN, elems), BF),
            pltpu.SemaphoreType.DMA((NV,)),
        ],
    )
    return residual, correction


def solution(mesh):
    split_last = P(None, None, ("gx", "gy"))
    flat = P(("gx", "gy"))
    return jax.shard_map(
        per_device,
        mesh=mesh,
        in_specs=(
            split_last,
            split_last,
            P(),
            P(),
            P(),
            flat,
            P(),
            flat,
            P(),
            P(("gx", "gy"), None),
            flat,
            split_last,
            P(),
            P(),
        ),
        out_specs=(split_last, split_last),
        check_vma=False,
    )
```

```python
import jax
import jax.numpy as jnp
from jax import lax
from jax.experimental import pallas as pl
from jax.experimental.pallas import tpu as pltpu
from jax.sharding import PartitionSpec as P

NV = 6
NN = 125
NF = 25
FR = 32
ASLOT = 32
MEMBERS = 8
RELAX = 0.7
WALL = 2.0
BF = jnp.bfloat16
F32 = jnp.float32
TOP = lax.Precision.HIGHEST
VMEM = pl.BlockSpec(memory_space=pltpu.VMEM)
HBM = pl.BlockSpec(memory_space=pltpu.HBM)
SMEM = pl.BlockSpec(memory_space=pltpu.SMEM)


def picker(faces, columns=NN):
    place = lax.broadcasted_iota(jnp.int32, (FR, columns), 0)
    node = lax.broadcasted_iota(jnp.int32, (FR, columns), 1)
    p, line = (node * 41) >> 10, (node * 205) >> 10
    q, r = line - 5 * p, node - 5 * line
    rows = []
    for face in faces:
        end = 4 * (face % 2)
        held, index = ((p, 5 * q + r), (q, 5 * p + r), (r, 5 * p + q))[face // 2]
        rows.append(((held == end) & (index == place) & (place < NF)).astype(F32))
    return jnp.concatenate(rows, axis=0).astype(BF)


def dot(a, b, **kw):
    return jnp.dot(a, b, preferred_element_type=F32, **kw)


def split(x):
    high = x.astype(BF)
    return high, (x - high.astype(F32)).astype(BF)


def call(kernel, outs, *args, scratch=(), smem=(), hbm_out=(), flops=1000, nbytes=1000):
    flat, tree = jax.tree.flatten(outs)
    return pl.pallas_call(
        kernel,
        out_shape=outs,
        in_specs=[SMEM if i in smem else VMEM for i in range(len(args))],
        out_specs=jax.tree.unflatten(tree, [HBM if i in hbm_out else VMEM for i in range(len(flat))]),
        scratch_shapes=list(scratch),
        compiler_params=pltpu.CompilerParams(vmem_limit_bytes=24 * 2**20),
        cost_estimate=pl.CostEstimate(flops=flops, bytes_accessed=nbytes, transcendentals=0),
    )(*args)


def is_odd():
    return lax.axis_index("gx") % 2 == 1


def faces_kernel(state, low_y, high_y, near_x, far_x):
    half = state.shape[2] // 2
    pick = picker((0, 1, 2, 3))
    odd = is_odd()
    for v in range(NV):
        found = dot(pick, state[v])
        low, high = found[:FR, :half], found[FR : 2 * FR, half:]
        far_x[v] = jnp.where(odd, high, low).astype(BF)
        near_x[v] = jnp.where(odd, low, high).astype(BF)
        low_y[v] = found[2 * FR : 3 * FR].astype(BF)
        high_y[v] = found[3 * FR :].astype(BF)


def halves(x):
    return [part.astype(F32) for part in split(x)]


def transposed_lifts(lift_t):
    gap = jnp.zeros((FR - NF, NN), F32)
    lifts = [jnp.concatenate([lift_t[f].astype(F32), gap], axis=0).T for f in range(6)]
    return jnp.concatenate(lifts, axis=1).astype(BF)


def weights_kernel(volume, viscous, lift_t, restrict, state_side, forcing_side, lift_side):
    both = jnp.concatenate(halves(restrict[...]), axis=0).astype(BF)

    def restricted(matrix):
        parts = dot(both, matrix)
        return halves(parts[:8] + parts[8:])

    lift_side[...] = jnp.concatenate(restricted(transposed_lifts(lift_t)), axis=0).astype(BF)
    forcing_side[...] = both
    parts = restricted(volume[...]) + restricted(viscous[...]) + halves(restrict[...])
    state_side[...] = jnp.concatenate([picker((0, 1, 4, 5)).astype(F32), *parts], axis=0).astype(BF)


def inverse_kernel(inverse, coupling, coarse_side):
    lanes = coarse_side.shape[2]
    rows, modes = inverse.shape[0] // 3, inverse.shape[2]
    blank = jnp.zeros((lanes - 3 * ASLOT, modes), F32)
    for r in range(rows):
        stacked = jnp.concatenate([inverse[r], inverse[rows + r], inverse[2 * rows + r], blank], axis=0)
        coarse_side[r] = RELAX * stacked.T
    coarse_side[rows] = jnp.concatenate([coupling[...], jnp.zeros((modes, lanes - modes), F32)], axis=1)


def restricted_kernel(mix, forcing, state, viscosity, flags, state_side, forcing_side, near, restricted):
    lanes = state.shape[2]
    half = lanes // 2
    place = lax.broadcasted_iota(jnp.int32, (FR, lanes), 1) % half
    visc = viscosity[...]
    fluxes, local = [], []
    for v in range(NV):
        found = dot(state_side[...], state[v])
        given = dot(forcing_side[...], forcing[v])
        t0, t1, t4, t5 = (found[FR * k : FR * (k + 1)] for k in range(4))
        across = t0[:, half:] - t1[:, :half]
        below = jnp.where(place == 0, 0.0, pltpu.roll(t5, 1, 1))
        above = jnp.where(place == half - 1, 0.0, pltpu.roll(t4, lanes - 1, 1))
        near[v, :FR] = jnp.concatenate([across, -across], axis=1).astype(BF)
        near[v, FR : 2 * FR] = (below - t4).astype(BF)
        near[v, 2 * FR :] = (above - t5).astype(BF)
        first = 4 * FR
        rows = [found[first + 16 * k : first + 16 * k + 8] + found[first + 16 * k + 8 : first + 16 * k + 16] for k in range(3)]
        total = given[:8] + given[8:] - visc * rows[1]
        if v == NV - 1:
            total = total - (WALL * flags[...].astype(F32)) * rows[2]
        fluxes.append(rows[0])
        local.append(total)
    for q in range(NV):
        total = local[q]
        for k in range(NV):
            total = total - mix[q, k] * fluxes[k]
        restricted[8 * q : 8 * q + 8] = total


def residual_kernel(
    mix, forcing, state, volume, viscous, viscosity, flags, lift_t, jumps, residual, done, flux, local, out, sems
):
    lifts = transposed_lifts(lift_t)
    for v in range(NV):
        u = state[v]
        flux[v, :NN] = dot(volume[...], u)
        total = forcing[v].astype(F32) - viscosity[...] * dot(viscous[...], u) + dot(lifts, jumps[v])
        if v == NV - 1:
            total = total - (WALL * flags[...].astype(F32)) * u.astype(F32)
        local[v] = total
    sends = []
    for q in range(NV):
        for low in range(0, NN, 16):
            rows = slice(low, min(low + 16, NN))
            total = local[q, rows]
            for k in range(NV):
                total = total - mix[q, k] * flux[k, rows]
            out[q, rows] = total.astype(BF)
        sends.append(pltpu.make_async_copy(out.at[q], residual.at[q], sems.at[q]))
        sends[-1].start()
    done[...] = jnp.zeros_like(done)
    for copy in sends:
        copy.wait()


def keys_of(owner, slot):
    return owner[...] * ASLOT + slot[...]


def one_hot(keys):
    groups = MEMBERS * ASLOT
    return (lax.broadcasted_iota(jnp.int32, (groups, keys.shape[1]), 0) == keys).astype(F32).astype(BF)


def sums_kernel(n1, n0, n2, n3, o2, o3, o1, o0, near, lift_side, restricted, owner, slot, blocks, jumps):
    half = owner.shape[1] // 2

    odd = is_odd()

    def difference(a, b):
        return a.astype(F32) - b.astype(F32)

    highs, lows = [], []
    for v in range(NV):
        far, close = difference(n0[v], o0[v]), difference(n1[v], o1[v])
        jumps[v, :FR, :half] = jnp.where(odd, close, far).astype(BF)
        jumps[v, :FR, half:] = near[v, :FR, half:]
        jumps[v, FR : 2 * FR, :half] = near[v, :FR, :half]
        jumps[v, FR : 2 * FR, half:] = jnp.where(odd, far, close).astype(BF)
        jumps[v, 2 * FR : 3 * FR] = difference(n2[v], o2[v]).astype(BF)
        jumps[v, 3 * FR : 4 * FR] = difference(n3[v], o3[v]).astype(BF)
        jumps[v, 4 * FR :] = near[v, FR:]
        both = dot(lift_side[...], jumps[v])
        high, low = halves(restricted[8 * v : 8 * v + 8] + both[:8] + both[8:])
        highs.append(high)
        lows.append(low)
    stacked = jnp.concatenate(highs + lows, axis=0).astype(BF)
    spread = one_hot(keys_of(owner, slot))
    both = lax.dot_general(stacked, spread, (((1,), (1,)), ((), ())), preferred_element_type=F32)
    sums = both[: 8 * NV] + both[8 * NV :]
    group = lax.broadcasted_iota(jnp.int32, (16, 128), 1) // ASLOT
    for m in range(MEMBERS):
        block = jnp.zeros((16, 128), F32)
        for k in range(3):
            piece = sums[16 * k : 16 * k + 16, (m // 4) * 128 : (m // 4 + 1) * 128]
            turn = ((k - m % 4) * ASLOT) % 128
            piece = pltpu.roll(piece, turn, 1) if turn else piece
            block = jnp.where(group == k, piece, block)
        blocks[m] = block


def opened(packed):
    group = lax.broadcasted_iota(jnp.int32, (16, 128), 1) // ASLOT
    rows = []
    for k in range(3):
        only = jnp.where(group == k, packed, 0.0)
        two = only + pltpu.roll(only, 32, 1)
        rows.append(two + pltpu.roll(two, 64, 1))
    return jnp.concatenate(rows, axis=0)


def solve(coarse_side, source, out):
    for r in range(16):
        out[r : r + 1] = jnp.sum(coarse_side[r] * source, axis=0, keepdims=True)


def first_kernel(blocks, coarse_side, _, totals, coarse):
    packed = jnp.sum(blocks[...], axis=0)
    source = opened(packed)
    totals[...] = source
    solve(coarse_side, source, coarse)


def sweep_kernel(up, down, totals, before, coarse_side, coarse):
    beside = opened(up[...] + down[...])
    coupling = coarse_side[16][:, : beside.shape[0]]
    source = totals[...] - dot(coupling, beside, precision=TOP)
    solve(coarse_side, source, coarse)
    coarse[...] = (1.0 - RELAX) * before[...] + coarse[...]


def last_sweep_kernel(up, down, totals, before, coarse_side, blocks, scratch):
    sweep_kernel(up, down, totals, before, coarse_side, scratch)
    for m in range(MEMBERS):
        blocks[m] = scratch[...]


def correction_kernel(blocks, prolong_t, owner, slot, correction, wide, out, sems):
    high, low = (x.astype(F32) for x in split(prolong_t[...]))
    weights = jnp.concatenate([high, low, high], axis=0)
    gap = jnp.zeros((weights.shape[0], wide.shape[0] // NV - NN), F32)
    weights = jnp.concatenate([weights, gap], axis=1).T.astype(BF)
    select = one_hot(keys_of(owner, slot))
    group = lax.broadcasted_iota(jnp.int32, (8, 128), 1) // ASLOT
    step = wide.shape[0] // NV
    for v in range(NV):
        k, rows = v // 2, slice(8 * (v % 2), 8 * (v % 2) + 8)
        parts = []
        for h in range(MEMBERS // 4):
            value = jnp.zeros((8, 128), F32)
            for w in range(4):
                turn = ((w - k) * ASLOT) % 128
                piece = blocks[4 * h + w, rows]
                piece = pltpu.roll(piece, turn, 1) if turn else piece
                value = jnp.where(group == w, piece, value)
            parts.append(value)
        high, low = (x.astype(F32) for x in split(jnp.concatenate(parts, axis=1)))
        values = jnp.concatenate([high, high, low], axis=0).astype(BF)
        wide[step * v : step * (v + 1)] = dot(weights, values).astype(BF)
    sends = []
    for first in range(0, NV, 2):
        found = dot(wide[step * first : step * (first + 2)], select)
        for v in (first, first + 1):
            out[v] = found[step * (v - first) : step * (v - first) + NN].astype(BF)
            sends.append(pltpu.make_async_copy(out.at[v], correction.at[v], sems.at[v]))
            sends[-1].start()
    for copy in sends:
        copy.wait()


def shifted(value, axis, by):
    size = lax.axis_size(axis)
    return lax.ppermute(value, axis, [(i, (i + by) % size) for i in range(size)])


def swapped(value, start):
    size = lax.axis_size("gx")
    return lax.ppermute(value, "gx", [(i, (i + (1 if i % 2 == start else -1)) % size) for i in range(size)])


def struct(shape, dtype):
    return jax.ShapeDtypeStruct(shape, dtype)


def per_device(
    state,
    forcing,
    volume_flux_matrix,
    viscous_matrix,
    linear_flux_matrix,
    viscosity,
    lift,
    wall_flags,
    restriction_weight,
    owner,
    slot,
    coarse_inverse,
    coupling,
    prolongation_weight,
):
    elems = state.shape[2]
    half = elems // 2
    owner, slot = owner.reshape(1, elems), slot.reshape(1, elems)
    viscosity, flags = viscosity.reshape(1, elems), wall_flags.reshape(1, elems)
    x_face, y_face = struct((NV, FR, half), BF), struct((NV, FR, elems), BF)
    field = struct((NV, NN, elems), BF)
    own = call(faces_kernel, (y_face, y_face, x_face, x_face), state, flops=2 * 10**10)
    far_x, near_x = swapped(own[3], 1), swapped(own[2], 0)
    restrict, inverse, _ = lax.optimization_barrier(
        (restriction_weight, jnp.transpose(coarse_inverse, (0, 2, 1)), own[0])
    )
    coarse_side = call(inverse_kernel, struct((17, 48, 128), F32), inverse, coupling)
    near = (near_x, far_x, shifted(own[1], "gy", 1), shifted(own[0], "gy", -1))
    lift_t = jnp.transpose(lift, (0, 2, 1))
    state_side, forcing_side, lift_side = call(
        weights_kernel,
        (struct((4 * FR + 48, NN), BF), struct((16, NN), BF), struct((16, 6 * FR), BF)),
        volume_flux_matrix,
        viscous_matrix,
        lift_t,
        restrict,
    )
    inner, restricted = call(
        restricted_kernel,
        (struct((NV, 3 * FR, elems), BF), struct((48, elems), F32)),
        linear_flux_matrix,
        forcing,
        state,
        viscosity,
        flags,
        state_side,
        forcing_side,
        smem=(0,),
    )
    restricted, coarse_side = lax.optimization_barrier((restricted, coarse_side))
    blocks, jumps = call(
        sums_kernel,
        (struct((MEMBERS, 16, 128), F32), struct((NV, 6 * FR, elems), BF)),
        *near,
        *own,
        inner,
        lift_side,
        restricted,
        owner,
        slot,
    )
    viscous_matrix, _ = lax.optimization_barrier((viscous_matrix, blocks))
    residual, done = call(
        residual_kernel,
        (field, struct((8, 128), F32)),
        linear_flux_matrix,
        forcing,
        state,
        volume_flux_matrix,
        viscous_matrix,
        viscosity,
        flags,
        lift_t,
        jumps,
        smem=(0,),
        hbm_out=(0,),
        scratch=[
            pltpu.VMEM((NV, 128, elems), F32),
            pltpu.VMEM((NV, NN, elems), F32),
            pltpu.VMEM((NV, NN, elems), BF),
            pltpu.SemaphoreType.DMA((NV,)),
        ],
    )
    blocks = lax.all_to_all(blocks, "gy", 0, 0, tiled=True)
    totals, coarse = call(
        first_kernel,
        (struct((48, 128), F32), struct((16, 128), F32)),
        blocks,
        coarse_side,
        done,
    )
    up, down = swapped(coarse, 0), swapped(coarse, 1)
    coarse = call(
        sweep_kernel, struct((16, 128), F32), up, down, totals, coarse, coarse_side, flops=5 * 10**9
    )
    up, down = swapped(coarse, 0), swapped(coarse, 1)
    blocks = call(
        last_sweep_kernel,
        struct((MEMBERS, 16, 128), F32),
        up,
        down,
        totals,
        coarse,
        coarse_side,
        scratch=[pltpu.VMEM((16, 128), F32)],
    )
    blocks = lax.all_to_all(blocks, "gy", 0, 0, tiled=True)
    correction = call(
        correction_kernel,
        field,
        blocks,
        jnp.transpose(prolongation_weight),
        owner,
        slot,
        hbm_out=(0,),
        scratch=[
            pltpu.VMEM((128 * NV, MEMBERS * ASLOT), BF),
            pltpu.VMEM((NV, NN, elems), BF),
            pltpu.SemaphoreType.DMA((NV,)),
        ],
    )
    return residual, correction


def solution(mesh):
    split_last = P(None, None, ("gx", "gy"))
    flat = P(("gx", "gy"))
    return jax.shard_map(
        per_device,
        mesh=mesh,
        in_specs=(
            split_last,
            split_last,
            P(),
            P(),
            P(),
            flat,
            P(),
            flat,
            P(),
            P(("gx", "gy"), None),
            flat,
            split_last,
            P(),
            P(),
        ),
        out_specs=(split_last, split_last),
        check_vma=False,
    )
```

```python
import jax
import jax.numpy as jnp
from jax import lax
from jax.experimental import pallas as pl
from jax.experimental.pallas import tpu as pltpu
from jax.sharding import PartitionSpec as P

NV = 6
NN = 125
NF = 25
FR = 32
ASLOT = 32
MEMBERS = 8
RELAX = 0.7
WALL = 2.0
BF = jnp.bfloat16
F32 = jnp.float32
TOP = lax.Precision.HIGHEST
VMEM = pl.BlockSpec(memory_space=pltpu.VMEM)
HBM = pl.BlockSpec(memory_space=pltpu.HBM)
SMEM = pl.BlockSpec(memory_space=pltpu.SMEM)


def picker(faces, columns=NN):
    place = lax.broadcasted_iota(jnp.int32, (FR, columns), 0)
    node = lax.broadcasted_iota(jnp.int32, (FR, columns), 1)
    p, line = (node * 41) >> 10, (node * 205) >> 10
    q, r = line - 5 * p, node - 5 * line
    rows = []
    for face in faces:
        end = 4 * (face % 2)
        held, index = ((p, 5 * q + r), (q, 5 * p + r), (r, 5 * p + q))[face // 2]
        rows.append(((held == end) & (index == place) & (place < NF)).astype(F32))
    return jnp.concatenate(rows, axis=0).astype(BF)


def dot(a, b, **kw):
    return jnp.dot(a, b, preferred_element_type=F32, **kw)


def split(x):
    high = x.astype(BF)
    return high, (x - high.astype(F32)).astype(BF)


def call(kernel, outs, *args, scratch=(), smem=(), hbm_out=(), flops=1000, nbytes=1000):
    flat, tree = jax.tree.flatten(outs)
    return pl.pallas_call(
        kernel,
        out_shape=outs,
        in_specs=[SMEM if i in smem else VMEM for i in range(len(args))],
        out_specs=jax.tree.unflatten(tree, [HBM if i in hbm_out else VMEM for i in range(len(flat))]),
        scratch_shapes=list(scratch),
        compiler_params=pltpu.CompilerParams(vmem_limit_bytes=24 * 2**20),
        cost_estimate=pl.CostEstimate(flops=flops, bytes_accessed=nbytes, transcendentals=0),
    )(*args)


def is_odd():
    return lax.axis_index("gx") % 2 == 1


def faces_kernel(state, low_y, high_y, near_x, far_x):
    half = state.shape[2] // 2
    pick = picker((0, 1, 2, 3))
    odd = is_odd()
    for v in range(NV):
        found = dot(pick, state[v])
        low, high = found[:FR, :half], found[FR : 2 * FR, half:]
        far_x[v] = jnp.where(odd, high, low).astype(BF)
        near_x[v] = jnp.where(odd, low, high).astype(BF)
        low_y[v] = found[2 * FR : 3 * FR].astype(BF)
        high_y[v] = found[3 * FR :].astype(BF)


def halves(x):
    return [part.astype(F32) for part in split(x)]


def transposed_lifts(lift_t):
    gap = jnp.zeros((FR - NF, NN), F32)
    lifts = [jnp.concatenate([lift_t[f].astype(F32), gap], axis=0).T for f in range(6)]
    return jnp.concatenate(lifts, axis=1).astype(BF)


def weights_kernel(volume, viscous, lift_t, restrict, state_side, forcing_side, lift_side):
    both = jnp.concatenate(halves(restrict[...]), axis=0).astype(BF)

    def restricted(matrix):
        parts = dot(both, matrix)
        return halves(parts[:8] + parts[8:])

    lift_side[...] = jnp.concatenate(restricted(transposed_lifts(lift_t)), axis=0).astype(BF)
    forcing_side[...] = both
    parts = restricted(volume[...]) + restricted(viscous[...]) + halves(restrict[...])
    state_side[...] = jnp.concatenate([picker((0, 1, 4, 5)).astype(F32), *parts], axis=0).astype(BF)


def inverse_kernel(inverse, coupling, coarse_side):
    lanes = coarse_side.shape[2]
    rows, modes = inverse.shape[0] // 3, inverse.shape[2]
    blank = jnp.zeros((lanes - 3 * ASLOT, modes), F32)
    for r in range(rows):
        stacked = jnp.concatenate([inverse[r], inverse[rows + r], inverse[2 * rows + r], blank], axis=0)
        coarse_side[r] = RELAX * stacked.T
    coarse_side[rows] = jnp.concatenate([coupling[...], jnp.zeros((modes, lanes - modes), F32)], axis=1)


def restricted_kernel(mix, forcing, state, viscosity, flags, state_side, forcing_side, near, restricted):
    lanes = state.shape[2]
    half = lanes // 2
    place = lax.broadcasted_iota(jnp.int32, (FR, lanes), 1) % half
    visc = viscosity[...]
    fluxes, local = [], []
    for v in range(NV):
        found = dot(state_side[...], state[v])
        given = dot(forcing_side[...], forcing[v])
        t0, t1, t4, t5 = (found[FR * k : FR * (k + 1)] for k in range(4))
        across = t0[:, half:] - t1[:, :half]
        below = jnp.where(place == 0, 0.0, pltpu.roll(t5, 1, 1))
        above = jnp.where(place == half - 1, 0.0, pltpu.roll(t4, lanes - 1, 1))
        near[v, :FR] = jnp.concatenate([across, -across], axis=1).astype(BF)
        near[v, FR : 2 * FR] = (below - t4).astype(BF)
        near[v, 2 * FR :] = (above - t5).astype(BF)
        first = 4 * FR
        rows = [found[first + 16 * k : first + 16 * k + 8] + found[first + 16 * k + 8 : first + 16 * k + 16] for k in range(3)]
        total = given[:8] + given[8:] - visc * rows[1]
        if v == NV - 1:
            total = total - (WALL * flags[...].astype(F32)) * rows[2]
        fluxes.append(rows[0])
        local.append(total)
    for q in range(NV):
        total = local[q]
        for k in range(NV):
            total = total - mix[q, k] * fluxes[k]
        restricted[8 * q : 8 * q + 8] = total


def products_kernel(forcing, state, volume, viscous, viscosity, flags, lift_t, jumps, flux, local, done):
    lifts = transposed_lifts(lift_t)
    for v in range(NV):
        u = state[v]
        flux[v, :NN] = dot(volume[...], u)
        total = forcing[v].astype(F32) - viscosity[...] * dot(viscous[...], u) + dot(lifts, jumps[v])
        if v == NV - 1:
            total = total - (WALL * flags[...].astype(F32)) * u.astype(F32)
        local[v] = total
    done[...] = jnp.zeros_like(done)


def mixed_kernel(mix, flux, local, residual, done, out, sems):
    sends = []
    for q in range(NV):
        for low in range(0, NN, 16):
            rows = slice(low, min(low + 16, NN))
            total = local[q, rows]
            for k in range(NV):
                total = total - mix[q, k] * flux[k, rows]
            out[q, rows] = total.astype(BF)
        sends.append(pltpu.make_async_copy(out.at[q], residual.at[q], sems.at[q]))
        sends[-1].start()
    done[...] = jnp.zeros_like(done)
    for copy in sends:
        copy.wait()


def keys_of(owner, slot):
    return owner[...] * ASLOT + slot[...]


def one_hot(keys):
    groups = MEMBERS * ASLOT
    return (lax.broadcasted_iota(jnp.int32, (groups, keys.shape[1]), 0) == keys).astype(F32).astype(BF)


def sums_kernel(n1, n0, n2, n3, o2, o3, o1, o0, near, lift_side, restricted, owner, slot, blocks, jumps):
    half = owner.shape[1] // 2

    odd = is_odd()

    def difference(a, b):
        return a.astype(F32) - b.astype(F32)

    highs, lows = [], []
    for v in range(NV):
        far, close = difference(n0[v], o0[v]), difference(n1[v], o1[v])
        jumps[v, :FR, :half] = jnp.where(odd, close, far).astype(BF)
        jumps[v, :FR, half:] = near[v, :FR, half:]
        jumps[v, FR : 2 * FR, :half] = near[v, :FR, :half]
        jumps[v, FR : 2 * FR, half:] = jnp.where(odd, far, close).astype(BF)
        jumps[v, 2 * FR : 3 * FR] = difference(n2[v], o2[v]).astype(BF)
        jumps[v, 3 * FR : 4 * FR] = difference(n3[v], o3[v]).astype(BF)
        jumps[v, 4 * FR :] = near[v, FR:]
        both = dot(lift_side[...], jumps[v])
        high, low = halves(restricted[8 * v : 8 * v + 8] + both[:8] + both[8:])
        highs.append(high)
        lows.append(low)
    stacked = jnp.concatenate(highs + lows, axis=0).astype(BF)
    spread = one_hot(keys_of(owner, slot))
    both = lax.dot_general(stacked, spread, (((1,), (1,)), ((), ())), preferred_element_type=F32)
    sums = both[: 8 * NV] + both[8 * NV :]
    group = lax.broadcasted_iota(jnp.int32, (16, 128), 1) // ASLOT
    for m in range(MEMBERS):
        block = jnp.zeros((16, 128), F32)
        for k in range(3):
            piece = sums[16 * k : 16 * k + 16, (m // 4) * 128 : (m // 4 + 1) * 128]
            turn = ((k - m % 4) * ASLOT) % 128
            piece = pltpu.roll(piece, turn, 1) if turn else piece
            block = jnp.where(group == k, piece, block)
        blocks[m] = block


def opened(packed):
    group = lax.broadcasted_iota(jnp.int32, (16, 128), 1) // ASLOT
    rows = []
    for k in range(3):
        only = jnp.where(group == k, packed, 0.0)
        two = only + pltpu.roll(only, 32, 1)
        rows.append(two + pltpu.roll(two, 64, 1))
    return jnp.concatenate(rows, axis=0)


def solve(coarse_side, source, out):
    for r in range(16):
        out[r : r + 1] = jnp.sum(coarse_side[r] * source, axis=0, keepdims=True)


def first_kernel(blocks, coarse_side, totals, coarse):
    packed = jnp.sum(blocks[...], axis=0)
    source = opened(packed)
    totals[...] = source
    solve(coarse_side, source, coarse)


def sweep_kernel(up, down, totals, before, coarse_side, _, coarse):
    beside = opened(up[...] + down[...])
    coupling = coarse_side[16][:, : beside.shape[0]]
    source = totals[...] - dot(coupling, beside, precision=TOP)
    solve(coarse_side, source, coarse)
    coarse[...] = (1.0 - RELAX) * before[...] + coarse[...]


def last_sweep_kernel(up, down, totals, before, coarse_side, _, blocks, scratch):
    sweep_kernel(up, down, totals, before, coarse_side, _, scratch)
    for m in range(MEMBERS):
        blocks[m] = scratch[...]


def correction_kernel(blocks, prolong_t, owner, slot, correction, wide, out, sems):
    high, low = (x.astype(F32) for x in split(prolong_t[...]))
    weights = jnp.concatenate([high, low, high], axis=0)
    gap = jnp.zeros((weights.shape[0], wide.shape[0] // NV - NN), F32)
    weights = jnp.concatenate([weights, gap], axis=1).T.astype(BF)
    select = one_hot(keys_of(owner, slot))
    group = lax.broadcasted_iota(jnp.int32, (8, 128), 1) // ASLOT
    step = wide.shape[0] // NV
    for v in range(NV):
        k, rows = v // 2, slice(8 * (v % 2), 8 * (v % 2) + 8)
        parts = []
        for h in range(MEMBERS // 4):
            value = jnp.zeros((8, 128), F32)
            for w in range(4):
                turn = ((w - k) * ASLOT) % 128
                piece = blocks[4 * h + w, rows]
                piece = pltpu.roll(piece, turn, 1) if turn else piece
                value = jnp.where(group == w, piece, value)
            parts.append(value)
        high, low = (x.astype(F32) for x in split(jnp.concatenate(parts, axis=1)))
        values = jnp.concatenate([high, high, low], axis=0).astype(BF)
        wide[step * v : step * (v + 1)] = dot(weights, values).astype(BF)
    sends = []
    for first in range(0, NV, 2):
        found = dot(wide[step * first : step * (first + 2)], select)
        for v in (first, first + 1):
            out[v] = found[step * (v - first) : step * (v - first) + NN].astype(BF)
            sends.append(pltpu.make_async_copy(out.at[v], correction.at[v], sems.at[v]))
            sends[-1].start()
    for copy in sends:
        copy.wait()


def shifted(value, axis, by):
    size = lax.axis_size(axis)
    return lax.ppermute(value, axis, [(i, (i + by) % size) for i in range(size)])


def swapped(value, start):
    size = lax.axis_size("gx")
    return lax.ppermute(value, "gx", [(i, (i + (1 if i % 2 == start else -1)) % size) for i in range(size)])


def struct(shape, dtype):
    return jax.ShapeDtypeStruct(shape, dtype)


def per_device(
    state,
    forcing,
    volume_flux_matrix,
    viscous_matrix,
    linear_flux_matrix,
    viscosity,
    lift,
    wall_flags,
    restriction_weight,
    owner,
    slot,
    coarse_inverse,
    coupling,
    prolongation_weight,
):
    elems = state.shape[2]
    half = elems // 2
    owner, slot = owner.reshape(1, elems), slot.reshape(1, elems)
    viscosity, flags = viscosity.reshape(1, elems), wall_flags.reshape(1, elems)
    x_face, y_face = struct((NV, FR, half), BF), struct((NV, FR, elems), BF)
    field = struct((NV, NN, elems), BF)
    own = call(faces_kernel, (y_face, y_face, x_face, x_face), state, flops=2 * 10**10)
    far_x, near_x = swapped(own[3], 1), swapped(own[2], 0)
    restrict, inverse, _ = lax.optimization_barrier(
        (restriction_weight, jnp.transpose(coarse_inverse, (0, 2, 1)), own[0])
    )
    coarse_side = call(inverse_kernel, struct((17, 48, 128), F32), inverse, coupling)
    near = (near_x, far_x, shifted(own[1], "gy", 1), shifted(own[0], "gy", -1))
    lift_t = jnp.transpose(lift, (0, 2, 1))
    state_side, forcing_side, lift_side = call(
        weights_kernel,
        (struct((4 * FR + 48, NN), BF), struct((16, NN), BF), struct((16, 6 * FR), BF)),
        volume_flux_matrix,
        viscous_matrix,
        lift_t,
        restrict,
    )
    inner, restricted = call(
        restricted_kernel,
        (struct((NV, 3 * FR, elems), BF), struct((48, elems), F32)),
        linear_flux_matrix,
        forcing,
        state,
        viscosity,
        flags,
        state_side,
        forcing_side,
        smem=(0,),
    )
    restricted, coarse_side = lax.optimization_barrier((restricted, coarse_side))
    blocks, jumps = call(
        sums_kernel,
        (struct((MEMBERS, 16, 128), F32), struct((NV, 6 * FR, elems), BF)),
        *near,
        *own,
        inner,
        lift_side,
        restricted,
        owner,
        slot,
    )
    blocks = lax.all_to_all(blocks, "gy", 0, 0, tiled=True)
    totals, coarse = call(
        first_kernel, (struct((48, 128), F32), struct((16, 128), F32)), blocks, coarse_side
    )
    far_c, near_c = swapped(coarse, 1), swapped(coarse, 0)
    mark = struct((8, 128), F32)
    lift_after, _ = lax.optimization_barrier((lift_t, coarse))
    flux, local, done = call(
        products_kernel,
        (struct((NV, 128, elems), F32), struct((NV, NN, elems), F32), mark),
        forcing,
        state,
        volume_flux_matrix,
        viscous_matrix,
        viscosity,
        flags,
        lift_after,
        jumps,
    )
    coarse = call(
        sweep_kernel, struct((16, 128), F32), far_c, near_c, totals, coarse, coarse_side, done
    )
    far_c, near_c = swapped(coarse, 1), swapped(coarse, 0)
    local, _ = lax.optimization_barrier((local, coarse))
    residual, done = call(
        mixed_kernel,
        (field, mark),
        linear_flux_matrix,
        flux,
        local,
        smem=(0,),
        hbm_out=(0,),
        scratch=[pltpu.VMEM((NV, NN, elems), BF), pltpu.SemaphoreType.DMA((NV,))],
    )
    blocks = call(
        last_sweep_kernel,
        struct((MEMBERS, 16, 128), F32),
        far_c,
        near_c,
        totals,
        coarse,
        coarse_side,
        done,
        scratch=[pltpu.VMEM((16, 128), F32)],
    )
    blocks = lax.all_to_all(blocks, "gy", 0, 0, tiled=True)
    correction = call(
        correction_kernel,
        field,
        blocks,
        jnp.transpose(prolongation_weight),
        owner,
        slot,
        hbm_out=(0,),
        scratch=[
            pltpu.VMEM((128 * NV, MEMBERS * ASLOT), BF),
            pltpu.VMEM((NV, NN, elems), BF),
            pltpu.SemaphoreType.DMA((NV,)),
        ],
    )
    return residual, correction


def solution(mesh):
    split_last = P(None, None, ("gx", "gy"))
    flat = P(("gx", "gy"))
    return jax.shard_map(
        per_device,
        mesh=mesh,
        in_specs=(
            split_last,
            split_last,
            P(),
            P(),
            P(),
            flat,
            P(),
            flat,
            P(),
            P(("gx", "gy"), None),
            flat,
            split_last,
            P(),
            P(),
        ),
        out_specs=(split_last, split_last),
        check_vma=False,
    )
```

```python
import jax
import jax.numpy as jnp
from jax import lax
from jax.experimental import pallas as pl
from jax.experimental.pallas import tpu as pltpu
from jax.sharding import PartitionSpec as P

NV = 6
NN = 125
NF = 25
FR = 32
ASLOT = 32
MEMBERS = 8
RELAX = 0.7
WALL = 2.0
BF = jnp.bfloat16
F32 = jnp.float32
TOP = lax.Precision.HIGHEST
VMEM = pl.BlockSpec(memory_space=pltpu.VMEM)
HBM = pl.BlockSpec(memory_space=pltpu.HBM)
SMEM = pl.BlockSpec(memory_space=pltpu.SMEM)


def picker(faces, columns=NN):
    place = lax.broadcasted_iota(jnp.int32, (FR, columns), 0)
    node = lax.broadcasted_iota(jnp.int32, (FR, columns), 1)
    p, line = (node * 41) >> 10, (node * 205) >> 10
    q, r = line - 5 * p, node - 5 * line
    rows = []
    for face in faces:
        end = 4 * (face % 2)
        held, index = ((p, 5 * q + r), (q, 5 * p + r), (r, 5 * p + q))[face // 2]
        rows.append(((held == end) & (index == place) & (place < NF)).astype(F32))
    return jnp.concatenate(rows, axis=0).astype(BF)


def dot(a, b, **kw):
    return jnp.dot(a, b, preferred_element_type=F32, **kw)


def split(x):
    high = x.astype(BF)
    return high, (x - high.astype(F32)).astype(BF)


def call(kernel, outs, *args, scratch=(), smem=(), hbm_out=(), flops=1000, nbytes=1000):
    flat, tree = jax.tree.flatten(outs)
    return pl.pallas_call(
        kernel,
        out_shape=outs,
        in_specs=[SMEM if i in smem else VMEM for i in range(len(args))],
        out_specs=jax.tree.unflatten(tree, [HBM if i in hbm_out else VMEM for i in range(len(flat))]),
        scratch_shapes=list(scratch),
        compiler_params=pltpu.CompilerParams(vmem_limit_bytes=24 * 2**20),
        cost_estimate=pl.CostEstimate(flops=flops, bytes_accessed=nbytes, transcendentals=0),
    )(*args)


def is_odd():
    return lax.axis_index("gx") % 2 == 1


def faces_kernel(state, low_y, high_y, near_x, far_x):
    half = state.shape[2] // 2
    pick = picker((0, 1, 2, 3))
    odd = is_odd()
    for v in range(NV):
        found = dot(pick, state[v])
        low, high = found[:FR, :half], found[FR : 2 * FR, half:]
        far_x[v] = jnp.where(odd, high, low).astype(BF)
        near_x[v] = jnp.where(odd, low, high).astype(BF)
        low_y[v] = found[2 * FR : 3 * FR].astype(BF)
        high_y[v] = found[3 * FR :].astype(BF)


def halves(x):
    return [part.astype(F32) for part in split(x)]


def transposed_lifts(lift_t):
    gap = jnp.zeros((FR - NF, NN), F32)
    lifts = [jnp.concatenate([lift_t[f].astype(F32), gap], axis=0).T for f in range(6)]
    return jnp.concatenate(lifts, axis=1).astype(BF)


def weights_kernel(volume, viscous, lift_t, restrict, state_side, forcing_side, lift_side):
    both = jnp.concatenate(halves(restrict[...]), axis=0).astype(BF)

    def restricted(matrix):
        parts = dot(both, matrix)
        return halves(parts[:8] + parts[8:])

    lift_side[...] = jnp.concatenate(restricted(transposed_lifts(lift_t)), axis=0).astype(BF)
    forcing_side[...] = both
    parts = restricted(volume[...]) + restricted(viscous[...]) + halves(restrict[...])
    state_side[...] = jnp.concatenate([picker((0, 1, 4, 5)).astype(F32), *parts], axis=0).astype(BF)


def inverse_kernel(inverse, coupling, coarse_side):
    lanes = coarse_side.shape[2]
    rows, modes = inverse.shape[0] // 3, inverse.shape[2]
    blank = jnp.zeros((lanes - 3 * ASLOT, modes), F32)
    for r in range(rows):
        stacked = jnp.concatenate([inverse[r], inverse[rows + r], inverse[2 * rows + r], blank], axis=0)
        coarse_side[r] = RELAX * stacked.T
    coarse_side[rows] = jnp.concatenate([coupling[...], jnp.zeros((modes, lanes - modes), F32)], axis=1)


def restricted_kernel(mix, forcing, state, viscosity, flags, state_side, forcing_side, near, restricted):
    lanes = state.shape[2]
    half = lanes // 2
    place = lax.broadcasted_iota(jnp.int32, (FR, lanes), 1) % half
    visc = viscosity[...]
    fluxes, local = [], []
    for v in range(NV):
        found = dot(state_side[...], state[v])
        given = dot(forcing_side[...], forcing[v])
        t0, t1, t4, t5 = (found[FR * k : FR * (k + 1)] for k in range(4))
        across = t0[:, half:] - t1[:, :half]
        below = jnp.where(place == 0, 0.0, pltpu.roll(t5, 1, 1))
        above = jnp.where(place == half - 1, 0.0, pltpu.roll(t4, lanes - 1, 1))
        near[v, :FR] = jnp.concatenate([across, -across], axis=1).astype(BF)
        near[v, FR : 2 * FR] = (below - t4).astype(BF)
        near[v, 2 * FR :] = (above - t5).astype(BF)
        first = 4 * FR
        rows = [found[first + 16 * k : first + 16 * k + 8] + found[first + 16 * k + 8 : first + 16 * k + 16] for k in range(3)]
        total = given[:8] + given[8:] - visc * rows[1]
        if v == NV - 1:
            total = total - (WALL * flags[...].astype(F32)) * rows[2]
        fluxes.append(rows[0])
        local.append(total)
    for q in range(NV):
        total = local[q]
        for k in range(NV):
            total = total - mix[q, k] * fluxes[k]
        restricted[8 * q : 8 * q + 8] = total


def products_kernel(forcing, state, volume, viscous, viscosity, flags, lift_t, jumps, flux, local, done):
    lifts = transposed_lifts(lift_t)
    for v in range(NV):
        u = state[v]
        flux[v, :NN] = dot(volume[...], u)
        total = forcing[v].astype(F32) - viscosity[...] * dot(viscous[...], u) + dot(lifts, jumps[v])
        if v == NV - 1:
            total = total - (WALL * flags[...].astype(F32)) * u.astype(F32)
        local[v] = total
    done[...] = jnp.zeros_like(done)


def mixed_kernel(mix, flux, local, owner, slot, residual, done, select, out, sems):
    select[...] = one_hot(keys_of(owner, slot))
    sends = []
    for q in range(NV):
        for low in range(0, NN, 16):
            rows = slice(low, min(low + 16, NN))
            total = local[q, rows]
            for k in range(NV):
                total = total - mix[q, k] * flux[k, rows]
            out[q, rows] = total.astype(BF)
        sends.append(pltpu.make_async_copy(out.at[q], residual.at[q], sems.at[q]))
        sends[-1].start()
    done[...] = jnp.zeros_like(done)
    for copy in sends:
        copy.wait()


def keys_of(owner, slot):
    return owner[...] * ASLOT + slot[...]


def one_hot(keys):
    groups = MEMBERS * ASLOT
    return (lax.broadcasted_iota(jnp.int32, (groups, keys.shape[1]), 0) == keys).astype(F32).astype(BF)


def sums_kernel(n1, n0, n2, n3, o2, o3, o1, o0, near, lift_side, restricted, owner, slot, blocks, jumps):
    half = owner.shape[1] // 2

    odd = is_odd()

    def difference(a, b):
        return a.astype(F32) - b.astype(F32)

    highs, lows = [], []
    for v in range(NV):
        far, close = difference(n0[v], o0[v]), difference(n1[v], o1[v])
        jumps[v, :FR, :half] = jnp.where(odd, close, far).astype(BF)
        jumps[v, :FR, half:] = near[v, :FR, half:]
        jumps[v, FR : 2 * FR, :half] = near[v, :FR, :half]
        jumps[v, FR : 2 * FR, half:] = jnp.where(odd, far, close).astype(BF)
        jumps[v, 2 * FR : 3 * FR] = difference(n2[v], o2[v]).astype(BF)
        jumps[v, 3 * FR : 4 * FR] = difference(n3[v], o3[v]).astype(BF)
        jumps[v, 4 * FR :] = near[v, FR:]
        both = dot(lift_side[...], jumps[v])
        high, low = halves(restricted[8 * v : 8 * v + 8] + both[:8] + both[8:])
        highs.append(high)
        lows.append(low)
    stacked = jnp.concatenate(highs + lows, axis=0).astype(BF)
    spread = one_hot(keys_of(owner, slot))
    both = lax.dot_general(stacked, spread, (((1,), (1,)), ((), ())), preferred_element_type=F32)
    sums = both[: 8 * NV] + both[8 * NV :]
    group = lax.broadcasted_iota(jnp.int32, (16, 128), 1) // ASLOT
    for m in range(MEMBERS):
        block = jnp.zeros((16, 128), F32)
        for k in range(3):
            piece = sums[16 * k : 16 * k + 16, (m // 4) * 128 : (m // 4 + 1) * 128]
            turn = ((k - m % 4) * ASLOT) % 128
            piece = pltpu.roll(piece, turn, 1) if turn else piece
            block = jnp.where(group == k, piece, block)
        blocks[m] = block


def opened(packed):
    group = lax.broadcasted_iota(jnp.int32, (16, 128), 1) // ASLOT
    rows = []
    for k in range(3):
        only = jnp.where(group == k, packed, 0.0)
        two = only + pltpu.roll(only, 32, 1)
        rows.append(two + pltpu.roll(two, 64, 1))
    return jnp.concatenate(rows, axis=0)


def solve(coarse_side, source, out):
    for r in range(16):
        out[r : r + 1] = jnp.sum(coarse_side[r] * source, axis=0, keepdims=True)


def first_kernel(blocks, coarse_side, totals, coarse):
    packed = jnp.sum(blocks[...], axis=0)
    source = opened(packed)
    totals[...] = source
    solve(coarse_side, source, coarse)


def sweep_kernel(up, down, totals, before, coarse_side, _, coarse):
    beside = opened(up[...] + down[...])
    coupling = coarse_side[16][:, : beside.shape[0]]
    source = totals[...] - dot(coupling, beside, precision=TOP)
    solve(coarse_side, source, coarse)
    coarse[...] = (1.0 - RELAX) * before[...] + coarse[...]


def last_sweep_kernel(up, down, totals, before, coarse_side, _, blocks, scratch):
    sweep_kernel(up, down, totals, before, coarse_side, _, scratch)
    for m in range(MEMBERS):
        blocks[m] = scratch[...]


def correction_kernel(blocks, prolong_t, select, correction, wide, out, sems):
    high, low = (x.astype(F32) for x in split(prolong_t[...]))
    weights = jnp.concatenate([high, low, high], axis=0)
    gap = jnp.zeros((weights.shape[0], wide.shape[0] // NV - NN), F32)
    weights = jnp.concatenate([weights, gap], axis=1).T.astype(BF)
    group = lax.broadcasted_iota(jnp.int32, (8, 128), 1) // ASLOT
    step = wide.shape[0] // NV
    for v in range(NV):
        k, rows = v // 2, slice(8 * (v % 2), 8 * (v % 2) + 8)
        parts = []
        for h in range(MEMBERS // 4):
            value = jnp.zeros((8, 128), F32)
            for w in range(4):
                turn = ((w - k) * ASLOT) % 128
                piece = blocks[4 * h + w, rows]
                piece = pltpu.roll(piece, turn, 1) if turn else piece
                value = jnp.where(group == w, piece, value)
            parts.append(value)
        high, low = (x.astype(F32) for x in split(jnp.concatenate(parts, axis=1)))
        values = jnp.concatenate([high, high, low], axis=0).astype(BF)
        wide[step * v : step * (v + 1)] = dot(weights, values).astype(BF)
    sends = []
    for first in range(0, NV, 2):
        found = dot(wide[step * first : step * (first + 2)], select[...])
        for v in (first, first + 1):
            out[v] = found[step * (v - first) : step * (v - first) + NN].astype(BF)
            sends.append(pltpu.make_async_copy(out.at[v], correction.at[v], sems.at[v]))
            sends[-1].start()
    for copy in sends:
        copy.wait()


def shifted(value, axis, by):
    size = lax.axis_size(axis)
    return lax.ppermute(value, axis, [(i, (i + by) % size) for i in range(size)])


def swapped(value, start):
    size = lax.axis_size("gx")
    return lax.ppermute(value, "gx", [(i, (i + (1 if i % 2 == start else -1)) % size) for i in range(size)])


def struct(shape, dtype):
    return jax.ShapeDtypeStruct(shape, dtype)


def per_device(
    state,
    forcing,
    volume_flux_matrix,
    viscous_matrix,
    linear_flux_matrix,
    viscosity,
    lift,
    wall_flags,
    restriction_weight,
    owner,
    slot,
    coarse_inverse,
    coupling,
    prolongation_weight,
):
    elems = state.shape[2]
    half = elems // 2
    owner, slot = owner.reshape(1, elems), slot.reshape(1, elems)
    viscosity, flags = viscosity.reshape(1, elems), wall_flags.reshape(1, elems)
    x_face, y_face = struct((NV, FR, half), BF), struct((NV, FR, elems), BF)
    field = struct((NV, NN, elems), BF)
    own = call(faces_kernel, (y_face, y_face, x_face, x_face), state, flops=2 * 10**10)
    far_x, near_x = swapped(own[3], 1), swapped(own[2], 0)
    restrict, inverse, _ = lax.optimization_barrier(
        (restriction_weight, jnp.transpose(coarse_inverse, (0, 2, 1)), own[0])
    )
    coarse_side = call(inverse_kernel, struct((17, 48, 128), F32), inverse, coupling)
    near = (near_x, far_x, shifted(own[1], "gy", 1), shifted(own[0], "gy", -1))
    lift_t = jnp.transpose(lift, (0, 2, 1))
    state_side, forcing_side, lift_side = call(
        weights_kernel,
        (struct((4 * FR + 48, NN), BF), struct((16, NN), BF), struct((16, 6 * FR), BF)),
        volume_flux_matrix,
        viscous_matrix,
        lift_t,
        restrict,
    )
    inner, restricted = call(
        restricted_kernel,
        (struct((NV, 3 * FR, elems), BF), struct((48, elems), F32)),
        linear_flux_matrix,
        forcing,
        state,
        viscosity,
        flags,
        state_side,
        forcing_side,
        smem=(0,),
    )
    restricted, coarse_side = lax.optimization_barrier((restricted, coarse_side))
    blocks, jumps = call(
        sums_kernel,
        (struct((MEMBERS, 16, 128), F32), struct((NV, 6 * FR, elems), BF)),
        *near,
        *own,
        inner,
        lift_side,
        restricted,
        owner,
        slot,
    )
    blocks = lax.all_to_all(blocks, "gy", 0, 0, tiled=True)
    totals, coarse = call(
        first_kernel, (struct((48, 128), F32), struct((16, 128), F32)), blocks, coarse_side
    )
    far_c, near_c = swapped(coarse, 1), swapped(coarse, 0)
    mark = struct((8, 128), F32)
    lift_after, _ = lax.optimization_barrier((lift_t, coarse))
    flux, local, done = call(
        products_kernel,
        (struct((NV, 128, elems), F32), struct((NV, NN, elems), F32), mark),
        forcing,
        state,
        volume_flux_matrix,
        viscous_matrix,
        viscosity,
        flags,
        lift_after,
        jumps,
    )
    coarse = call(
        sweep_kernel, struct((16, 128), F32), far_c, near_c, totals, coarse, coarse_side, done
    )
    far_c, near_c = swapped(coarse, 1), swapped(coarse, 0)
    local, _ = lax.optimization_barrier((local, coarse))
    residual, done, select = call(
        mixed_kernel,
        (field, mark, struct((MEMBERS * ASLOT, elems), BF)),
        linear_flux_matrix,
        flux,
        local,
        owner,
        slot,
        smem=(0,),
        hbm_out=(0,),
        scratch=[pltpu.VMEM((NV, NN, elems), BF), pltpu.SemaphoreType.DMA((NV,))],
    )
    blocks = call(
        last_sweep_kernel,
        struct((MEMBERS, 16, 128), F32),
        far_c,
        near_c,
        totals,
        coarse,
        coarse_side,
        done,
        scratch=[pltpu.VMEM((16, 128), F32)],
    )
    blocks = lax.all_to_all(blocks, "gy", 0, 0, tiled=True)
    correction = call(
        correction_kernel,
        field,
        blocks,
        jnp.transpose(prolongation_weight),
        select,
        hbm_out=(0,),
        scratch=[
            pltpu.VMEM((128 * NV, MEMBERS * ASLOT), BF),
            pltpu.VMEM((NV, NN, elems), BF),
            pltpu.SemaphoreType.DMA((NV,)),
        ],
    )
    return residual, correction


def solution(mesh):
    split_last = P(None, None, ("gx", "gy"))
    flat = P(("gx", "gy"))
    return jax.shard_map(
        per_device,
        mesh=mesh,
        in_specs=(
            split_last,
            split_last,
            P(),
            P(),
            P(),
            flat,
            P(),
            flat,
            P(),
            P(("gx", "gy"), None),
            flat,
            split_last,
            P(),
            P(),
        ),
        out_specs=(split_last, split_last),
        check_vma=False,
    )
```
